128 devices in a mesh: kv: 16 (over y, x), head: 8 (over z, core).
Axes of the slice: x: 4, y: 4, z: 4, core: 2. Of those that a mesh axis runs over, the one named last changes fastest.
Arguments:
- tokens: bfloat16 [128, 5120], P(None, 'kv'), may hold values from -6 to 6
- q_weight: bfloat16 [5120, 8192], P('kv', 'head'), may hold values from -0.078125 to 0.078125
- key_matrix: bfloat16 [5120, 1024], P('kv', 'head'), may hold values from -0.078125 to 0.078125
- value_matrix: bfloat16 [5120, 1024], P('kv', 'head'), may hold values from -0.078125 to 0.078125
- q_gain: float32 [64, 128], P('head'), may hold values from 0.4 to 45, as said below
- key_norm_scale: float32 [8, 128], P('head'), may hold values from 0.4 to 1.8
- stored_cache_keys: bfloat16 [32, 16384, 8, 128], P(None, 'kv', 'head'), may hold values from -6 to 6
- stored_cache_values: bfloat16 [32, 16384, 8, 128], P(None, 'kv', 'head'), may hold values from -6 to 6
- lengths: int32 [32], replicated, may hold values from 8 to 16384, as said below
- positions: int32 [32, 4], replicated, may hold values from 8 to 16387, as said below
- o_weight: bfloat16 [8192, 5120], P('head', 'kv'), may hold values from -0.0625 to 0.0625
Outputs:
- layer_out: bfloat16 [128, 5120], P('head', 'kv')
The draws below stay inside these ranges and needn't reach their ends.
Inputs may be any that keep to these rules, and one draw needn't show every extreme that they name: `lengths`: every length is 8 or more; one request in each draw has exactly 16384 live positions. positions[r, 0] = lengths[r], and each later draft's position equals the previous one's or exceeds it by one; the request with 16384 live positions has its drafts at consecutive positions. `q_gain`: positive scales.
All inputs are finite; a program needn't handle non-finite values.
Results may differ from the reference program's by a relative error of at most 0.015.
Values may be sent and summed in bfloat16 or wider, within the bound.
A program may use at most 128 MiB of HBM per device.

```python
import math
import jax
import jax.numpy as jnp
from jax import lax

MODEL_WIDTH = 5120
QUERY_HEADS = 64
KEY_VALUE_HEADS = 8
HEAD_SIZE = 128
DRAFT_TOKENS = 4
REQUEST_COUNT = 32
CACHE_LENGTH = 16384
ROWS = 128


def lengths_and_places(key):
    base = jax.random.fold_in(key, 7)
    key_exp, key_off, key_pick, key_step = jax.random.split(base, 4)
    top_bit = CACHE_LENGTH.bit_length() - 1
    exponent = jax.random.randint(key_exp, (REQUEST_COUNT,), 3, top_bit)
    lowest = jnp.left_shift(jnp.ones((REQUEST_COUNT,), jnp.int32), exponent.astype(jnp.int32))
    length = jax.random.randint(key_off, (REQUEST_COUNT,), lowest, 2 * lowest)
    picked = jax.random.randint(key_pick, (), 0, REQUEST_COUNT)
    chosen = jnp.arange(REQUEST_COUNT) == picked
    length = jnp.where(chosen, CACHE_LENGTH, length).astype(jnp.int32)
    steps = jax.random.randint(key_step, (REQUEST_COUNT, DRAFT_TOKENS - 1), 0, 2)
    steps = jnp.where(chosen[:, None], 1, steps).astype(jnp.int32)
    depth = jnp.concatenate([jnp.zeros((REQUEST_COUNT, 1), jnp.int32), jnp.cumsum(steps, axis=1).astype(jnp.int32)], axis=1)
    return (length, (length[:, None] + depth).astype(jnp.int32))


def draw_lengths(key, part):
    return lengths_and_places(key)[0]


def draw_positions(key, part):
    return lengths_and_places(key)[1]


def draw_q_gain(key, part):
    return jax.random.uniform(key, (QUERY_HEADS, HEAD_SIZE), jnp.float32, 0.4, 1.8)


def level_of(stream_key, dims, shards, least, top_value):
    def one(axis_at, shards_of):
        heights = jax.random.uniform(jax.random.fold_in(jax.random.fold_in(stream_key, 6), axis_at), (shards_of,), jnp.float32, least / len(shards), top_value / len(shards))
        return jnp.repeat(jnp.exp(heights), dims[axis_at] // shards_of).reshape((-1,) + (1,) * (len(dims) - axis_at - 1))

    loudness = one(*shards[0])
    for cut in shards[1:]:
        loudness = loudness * one(*cut)
    return loudness


def bell_draw(stream_key, shape, scale, reach, cuts=(), held_as=jnp.bfloat16):
    level = level_of(stream_key, shape, cuts, -0.22, 0.18) if cuts else 1.0
    entries = jax.random.normal(stream_key, shape, jnp.float32) * scale * level
    return jnp.minimum(jnp.maximum(entries, -reach), reach).astype(held_as)


def setup_inputs(seed: int = 0) -> dict:
    streams_of = jax.random.split(jax.random.key(seed), 12)
    return {
        "tokens": bell_draw(streams_of[0], (ROWS, MODEL_WIDTH), 1.0, 6.0, ((1, 16),)),
        "q_weight": bell_draw(streams_of[1], (MODEL_WIDTH, QUERY_HEADS * HEAD_SIZE), MODEL_WIDTH ** -0.5, 0.078125, ((0, 16), (1, 8))),
        "key_matrix": bell_draw(streams_of[2], (MODEL_WIDTH, KEY_VALUE_HEADS * HEAD_SIZE), MODEL_WIDTH ** -0.5, 0.078125, ((0, 16), (1, 8))),
        "value_matrix": bell_draw(streams_of[3], (MODEL_WIDTH, KEY_VALUE_HEADS * HEAD_SIZE), MODEL_WIDTH ** -0.5, 0.078125, ((0, 16), (1, 8))),
        "q_gain": draw_q_gain(jax.random.fold_in(streams_of[11], 71), 0),
        "key_norm_scale": jnp.clip(0.4 + 1.4 * jax.random.uniform(streams_of[5], (KEY_VALUE_HEADS, HEAD_SIZE), jnp.float32) ** level_of(streams_of[5], (KEY_VALUE_HEADS, HEAD_SIZE), ((0, 8),), -0.2, 0.2), 0.4, 1.8),
        "stored_cache_keys": bell_draw(streams_of[6], (REQUEST_COUNT, CACHE_LENGTH, KEY_VALUE_HEADS, HEAD_SIZE), 1.0, 6.0, ((1, 16), (2, 8))),
        "stored_cache_values": bell_draw(streams_of[7], (REQUEST_COUNT, CACHE_LENGTH, KEY_VALUE_HEADS, HEAD_SIZE), 1.0, 6.0, ((1, 16), (2, 8))),
        "lengths": draw_lengths(jax.random.fold_in(streams_of[11], 71), 0),
        "positions": draw_positions(jax.random.fold_in(streams_of[11], 71), 0),
        "o_weight": bell_draw(streams_of[10], (QUERY_HEADS * HEAD_SIZE, MODEL_WIDTH), (QUERY_HEADS * HEAD_SIZE) ** -0.5, 0.0625, ((0, 8), (1, 16))),
    }


EPSILON = 1e-06
ROPE_BASE = 1000000.0
NEG = -1e+30

def norm_rotate(proj, gain, pos_rows):
    heads, head_dim = gain.shape
    count = proj.shape[0]
    vec = proj.reshape(count, heads, head_dim)
    vec = vec * lax.rsqrt(lax.optimization_barrier(jnp.mean(vec * vec, axis=-1, keepdims=True)) + EPSILON) * gain
    half = head_dim // 2
    freq = ROPE_BASE ** (-(jnp.arange(half, dtype=jnp.float32) * 2.0 / head_dim))
    angle = pos_rows.astype(jnp.float32)[:, None, None] * freq
    cosine = jnp.cos(angle)
    sine = jnp.sin(angle)
    first = vec[..., :half]
    second = vec[..., half:]
    out = jnp.concatenate([first * cosine - second * sine, second * cosine + first * sine], axis=-1)
    return out.reshape(count, heads * head_dim).astype(jnp.bfloat16)

def reference(tokens, q_weight, key_matrix, value_matrix, q_gain, key_norm_scale, stored_cache_keys, stored_cache_values, lengths, positions, o_weight):
    rows = tokens.shape[0]
    pos_rows = positions.reshape(rows)
    query_rows = norm_rotate(jnp.dot(tokens, q_weight, preferred_element_type=jnp.float32), q_gain, pos_rows)
    incoming_keys = norm_rotate(jnp.dot(tokens, key_matrix, preferred_element_type=jnp.float32), key_norm_scale, pos_rows)
    incoming_values = jnp.dot(tokens, value_matrix, preferred_element_type=jnp.float32).astype(jnp.bfloat16)
    group_size = QUERY_HEADS // KEY_VALUE_HEADS
    query_heads_full = query_rows.reshape(REQUEST_COUNT, DRAFT_TOKENS, KEY_VALUE_HEADS, group_size, HEAD_SIZE)
    draft_key_rows = incoming_keys.reshape(REQUEST_COUNT, DRAFT_TOKENS, KEY_VALUE_HEADS, HEAD_SIZE)
    draft_value_rows = incoming_values.reshape(REQUEST_COUNT, DRAFT_TOKENS, KEY_VALUE_HEADS, HEAD_SIZE)

    def one_request(items):
        query, keys, values, new_keys, new_values, length, place = items
        keys_all = jnp.concatenate([keys, new_keys], axis=0).astype(jnp.float32)
        values_all = jnp.concatenate([values, new_values], axis=0).astype(jnp.float32)
        scores = jnp.einsum('jkgd,tkd->jkgt', query.astype(jnp.float32), keys_all, precision=lax.Precision.HIGHEST) / math.sqrt(HEAD_SIZE)
        cache_live = jnp.arange(CACHE_LENGTH, dtype=jnp.int32) < length
        order = jnp.arange(DRAFT_TOKENS, dtype=jnp.int32)
        draft_live = (order[None, :] == order[:, None]) | (order[None, :] < order[:, None]) & (place[None, :] < place[:, None])
        live = jnp.concatenate([jnp.broadcast_to(cache_live[None, :], (DRAFT_TOKENS, CACHE_LENGTH)), draft_live], axis=1)
        mask = live[:, None, None, :]
        top = lax.optimization_barrier(jnp.max(jnp.where(mask, scores, NEG), axis=-1, keepdims=True))
        weights = jnp.where(mask, jnp.exp(scores - top), 0.0)
        total = lax.optimization_barrier(jnp.sum(weights, axis=-1))
        rounded = lax.optimization_barrier(weights.astype(jnp.bfloat16))
        acc = jnp.einsum('jkgt,tkd->jkgd', rounded.astype(jnp.float32), values_all, precision=lax.Precision.HIGHEST)
        return (acc / total[..., None]).astype(jnp.bfloat16)
    attended = lax.map(one_request, (query_heads_full, stored_cache_keys, stored_cache_values, draft_key_rows, draft_value_rows, lengths, positions))
    attended = attended.reshape(rows, QUERY_HEADS * HEAD_SIZE)
    return jnp.dot(attended, o_weight, preferred_element_type=jnp.float32).astype(jnp.bfloat16)
```

```python
import functools
import math

import jax
import jax.numpy as jnp
import numpy as np
from jax import lax
from jax.experimental import pallas as pl
from jax.experimental.pallas import tpu as pltpu
from jax.sharding import PartitionSpec as P

EPSILON = 1e-06
ROPE_BASE = 1000000.0
NEG = -1e30
MESH = pl.DeviceIdType.MESH


def column_to_row(col):
    rows = col.shape[0]
    wide = jnp.broadcast_to(col, (rows, 128))
    row_id = lax.broadcasted_iota(jnp.int32, (rows, 128), 0)
    lane_id = lax.broadcasted_iota(jnp.int32, (rows, 128), 1)
    return jnp.sum(jnp.where(row_id == lane_id, wide, 0.0), axis=0, keepdims=True)


def kernel(
    nk, side, nh, drafts,
    tokens, q_weight, key_matrix, value_matrix, q_gain, k_gain, keys, values, o_weight, freq,
    lengths, positions,
    out,
    tok_v, wq_v, wk_v, wv_v, qg_v, kg_v, wo_v, freq_v, keys_v, values_v,
    part, part_in, query, attn, attn_in, lse, lse_in, attended, proj, proj_in,
    load_sem, key_sem, value_sem, part_ss, part_rs, query_ss, query_rs,
    attn_ss, attn_rs, lse_ss, lse_rs, att_ss, att_rs, proj_ss, proj_rs,
):
    me = lax.axis_index("kv")
    my_head = lax.axis_index("head")
    my_y, my_x = me // side, me % side
    reqs, local_len, head_dim = keys.shape
    rows = tokens.shape[1]
    heads = q_gain.shape[0]
    per = reqs // nk
    own = per * drafts
    group = heads * drafts
    scale = 1.0 / math.sqrt(head_dim)
    to_log2 = scale * math.log2(math.e)

    def ahead(s):
        return lax.rem(my_y + s // side, side) * side + lax.rem(my_x + s % side, side)

    def behind(s):
        return (
            lax.rem(my_y + side - s // side, side) * side + lax.rem(my_x + side - s % side, side)
        )

    barrier = pltpu.get_barrier_semaphore()
    for s in range(1, nk):
        pl.semaphore_signal(barrier, inc=1, device_id={"kv": ahead(s)}, device_id_type=MESH)
    for s in range(1, nh):
        pl.semaphore_signal(
            barrier, inc=1, device_id={"head": lax.rem(my_head + s, nh)}, device_id_type=MESH
        )

    loads = [
        pltpu.make_async_copy(src, dst, load_sem.at[n])
        for n, (src, dst) in enumerate(
            [
                (tokens, tok_v), (q_weight, wq_v), (key_matrix, wk_v), (value_matrix, wv_v),
                (q_gain, qg_v), (k_gain, kg_v), (freq, freq_v), (o_weight, wo_v),
            ]
        )
    ]
    for copy in loads:
        copy.start()

    def cache_copies(s):
        at = pl.ds(per * behind(s), per)
        slot = pl.ds(per * s, per)
        return (
            pltpu.make_async_copy(keys.at[at], keys_v.at[slot], key_sem.at[s]),
            pltpu.make_async_copy(values.at[at], values_v.at[slot], value_sem.at[s]),
        )

    @pl.loop(0, nk)
    def _(s):
        for copy in cache_copies(s):
            copy.start()

    for copy in loads[:4]:
        copy.wait()
    toks = tok_v[...]
    for h in range(heads + 2):
        if h < heads:
            weight = wq_v[:, h * head_dim : (h + 1) * head_dim]
        else:
            weight = (wk_v if h == heads else wv_v)[...]
        part[:, h * own : (h + 1) * own, :] = lax.dot_general(
            toks, weight, (((0,), (0,)), ((), ())), preferred_element_type=jnp.float32
        ).reshape(nk, own, head_dim)

    pl.semaphore_wait(barrier, nk + nh - 2)

    def part_copy(s):
        return pltpu.make_async_remote_copy(
            src_ref=part.at[ahead(s)], dst_ref=part_in.at[s],
            send_sem=part_ss.at[s], recv_sem=part_rs.at[s],
            device_id={"kv": ahead(s)}, device_id_type=MESH,
        )

    @pl.loop(1, nk)
    def _(s):
        part_copy(s).start()

    for copy in loads[4:]:
        copy.wait()
    row_id = lax.broadcasted_iota(jnp.int32, (own, head_dim), 0)
    lane_id = lax.broadcasted_iota(jnp.int32, (own, head_dim), 1)
    place = [[positions[j, per * me + r] for j in range(drafts)] for r in range(per)]
    place_rows = jnp.zeros((own, head_dim), jnp.int32)
    for r in range(per):
        for j in range(drafts):
            place_rows = jnp.where(row_id == r * drafts + j, place[r][j], place_rows)
    angle = place_rows.astype(jnp.float32) * freq_v[...]
    cosine = jnp.cos(angle)
    sine = jnp.sin(angle)
    sine = jnp.where(lane_id < head_dim // 2, -sine, sine)
    fresh_row = lax.broadcasted_iota(jnp.int32, (per * group, 16), 0)
    fresh_col = lax.broadcasted_iota(jnp.int32, (per * group, 16), 1)
    seen = fresh_row < 0
    for r in range(per):
        for j in range(drafts):
            here = (fresh_row // group == r) & (fresh_row % drafts == j)
            for i in range(j + 1):
                hit = here & (fresh_col == r * drafts + i)
                if i < j:
                    hit = hit & (place[r][i] < place[r][j])
                seen = seen | hit

    @pl.loop(1, nk)
    def _(s):
        part_copy(s).wait_recv()

    raw = part[me]
    for s in range(1, nk):
        raw = raw + part_in[s]
    raw = raw.reshape(heads + 2, own, head_dim)

    def norm_rotate(vec, gain):
        vec = vec * lax.rsqrt(jnp.mean(vec * vec, axis=-1, keepdims=True) + EPSILON) * gain
        turned = pltpu.roll(vec.reshape(-1, head_dim), head_dim // 2, 1).reshape(vec.shape)
        return vec * cosine[None] + turned * sine[None]

    queries = norm_rotate(raw[:heads], qg_v[...][:, None, :])
    queries = jnp.swapaxes(queries.reshape(heads, per, drafts, head_dim), 0, 1)
    queries = queries.reshape(per * group, head_dim).astype(jnp.bfloat16)
    query[0] = queries

    def query_copy(s):
        return pltpu.make_async_remote_copy(
            src_ref=query.at[0], dst_ref=query.at[s],
            send_sem=query_ss.at[s], recv_sem=query_rs.at[s],
            device_id={"kv": ahead(s)}, device_id_type=MESH,
        )

    @pl.loop(1, nk)
    def _(s):
        query_copy(s).start()

    fresh_k = norm_rotate(raw[heads : heads + 1], kg_v[...][:, None, :]).reshape(own, head_dim)
    pad = jnp.zeros((16 - own, head_dim), jnp.float32)
    fresh_k = jnp.concatenate([fresh_k, pad], axis=0).astype(jnp.bfloat16)
    fresh_v = jnp.concatenate([raw[heads + 1], pad], axis=0).astype(jnp.bfloat16)

    def softmax_part(scores, vals):
        top = jnp.max(scores, axis=-1, keepdims=True)
        weights = jnp.exp2((scores - top) * to_log2)
        total = jnp.sum(weights, axis=-1, keepdims=True)
        mixed = jnp.dot(weights.astype(jnp.bfloat16), vals, preferred_element_type=jnp.float32)
        return mixed / total, top * to_log2 + jnp.log2(total)

    def dot_t(left, right):
        return lax.dot_general(
            left, right, (((1,), (1,)), ((), ())), preferred_element_type=jnp.float32
        )

    fresh_out, fresh_lse = softmax_part(
        jnp.where(seen, dot_t(queries, fresh_k), NEG), fresh_v
    )
    fresh_lse = column_to_row(fresh_lse)

    def attn_copies(s):
        return (
            pltpu.make_async_remote_copy(
                src_ref=attn.at[s], dst_ref=attn_in.at[s],
                send_sem=attn_ss.at[s], recv_sem=attn_rs.at[s],
                device_id={"kv": behind(s)}, device_id_type=MESH,
            ),
            pltpu.make_async_remote_copy(
                src_ref=lse.at[s], dst_ref=lse_in.at[s],
                send_sem=lse_ss.at[s], recv_sem=lse_rs.at[s],
                device_id={"kv": behind(s)}, device_id_type=MESH,
            ),
        )

    spot = me * local_len + lax.broadcasted_iota(jnp.int32, (1, local_len), 1)

    @pl.loop(0, nk)
    def _(s):
        @pl.when(s > 0)
        def _():
            query_copy(s).wait_recv()

        for copy in cache_copies(s):
            copy.wait()
        block = query[s]
        outs, stats = [], []
        for r in range(per):
            live = spot < lengths[per * behind(s) + r]
            scores = dot_t(block[r * group : (r + 1) * group], keys_v[per * s + r])
            mixed, stat = softmax_part(jnp.where(live, scores, NEG), values_v[per * s + r])
            outs.append(mixed)
            stats.append(stat)
        attn[s] = jnp.concatenate(outs, axis=0).astype(jnp.bfloat16)
        lse[s] = column_to_row(jnp.concatenate(stats, axis=0))

        @pl.when(s > 0)
        def _():
            for copy in attn_copies(s):
                copy.start()

    @pl.loop(1, nk)
    def _(s):
        for copy in attn_copies(s):
            copy.wait_recv()

    stats = jnp.concatenate([lse[0], fresh_lse] + [lse_in[s] for s in range(1, nk)], axis=0)
    ratio = jnp.exp2(stats - jnp.max(stats, axis=0, keepdims=True))
    ratio = ratio / jnp.sum(ratio, axis=0, keepdims=True)
    ratio = jnp.concatenate([ratio, jnp.zeros((128 - nk - 1, 128), jnp.float32)], axis=0).T
    ratio = ratio[: per * group]
    merged = attn[0].astype(jnp.float32) * ratio[:, 0:1] + fresh_out * ratio[:, 1:2]
    for s in range(1, nk):
        merged = merged + attn_in[s].astype(jnp.float32) * ratio[:, s + 1 : s + 2]
    merged = jnp.swapaxes(merged.reshape(per, heads, drafts, head_dim), 0, 1)
    attended[me] = merged.reshape(heads * own, head_dim).astype(jnp.bfloat16)

    def att_copy(s):
        return pltpu.make_async_remote_copy(
            src_ref=attended.at[me], dst_ref=attended.at[me],
            send_sem=att_ss.at[s], recv_sem=att_rs.at[s],
            device_id={"kv": ahead(s)}, device_id_type=MESH,
        )

    def att_arrival(s):
        return pltpu.make_async_remote_copy(
            src_ref=attended.at[me], dst_ref=attended.at[behind(s)],
            send_sem=att_ss.at[s], recv_sem=att_rs.at[s],
            device_id={"kv": ahead(s)}, device_id_type=MESH,
        )

    @pl.loop(1, nk)
    def _(s):
        att_copy(s).start()

    @pl.loop(1, nk)
    def _(s):
        att_arrival(s).wait_recv()

    total = None
    for h in range(0, heads, 2):
        pair = attended[:, h * own : (h + 2) * own, :].astype(jnp.float32)
        pair = pair.reshape(nk, 2, own, head_dim)
        for k in range(2):
            side_in = pair[:, k].reshape(rows, head_dim).astype(jnp.bfloat16)
            term = dot_t(side_in, wo_v[:, (h + k) * head_dim : (h + k + 1) * head_dim])
            total = term if total is None else total + term
    proj[...] = total.astype(jnp.bfloat16).reshape(proj.shape)

    def proj_copy(s):
        target = lax.rem(my_head + s, nh)
        return pltpu.make_async_remote_copy(
            src_ref=proj.at[target], dst_ref=proj_in.at[s],
            send_sem=proj_ss.at[s], recv_sem=proj_rs.at[s],
            device_id={"head": target}, device_id_type=MESH,
        )

    for s in range(1, nh):
        proj_copy(s).start()
    for s in range(1, nh):
        proj_copy(s).wait_recv()
    result = proj[my_head].astype(jnp.float32)
    for s in range(1, nh):
        result = result + proj_in[s].astype(jnp.float32)
    out[...] = result.astype(jnp.bfloat16)

    @pl.loop(1, nk)
    def _(s):
        part_copy(s).wait_send()
        query_copy(s).wait_send()
        for copy in attn_copies(s):
            copy.wait_send()
        att_copy(s).wait_send()

    for s in range(1, nh):
        proj_copy(s).wait_send()


def on_device(
    nk, nh,
    tokens, q_weight, key_matrix, value_matrix, q_gain, k_gain, keys, values, lengths, positions,
    o_weight,
):
    rows = tokens.shape[0]
    reqs, drafts = positions.shape
    width = o_weight.shape[1]
    tokens, o_weight, positions = tokens.T, o_weight.T, positions.T
    _, local_len, _, head_dim = keys.shape
    keys = keys.reshape(reqs, local_len, head_dim)
    values = values.reshape(reqs, local_len, head_dim)
    heads = q_gain.shape[0]
    side = math.isqrt(nk)
    own = rows // nk
    block = rows // nh
    exponent = np.arange(head_dim // 2, dtype=np.float64) * 2.0 / head_dim
    freq = np.tile((ROPE_BASE ** -exponent).astype(np.float32), 2)[None]
    bf16, f32 = jnp.bfloat16, jnp.float32
    dma = pltpu.SemaphoreType.DMA
    hbm = pl.BlockSpec(memory_space=pltpu.HBM)
    smem = pl.BlockSpec(memory_space=pltpu.SMEM)
    return pl.pallas_call(
        functools.partial(kernel, nk, side, nh, drafts),
        out_shape=jax.ShapeDtypeStruct((block, width), bf16),
        in_specs=[hbm] * 10 + [smem] * 2,
        out_specs=pl.BlockSpec(memory_space=pltpu.VMEM),
        scratch_shapes=[
            pltpu.VMEM(tokens.shape, bf16),
            pltpu.VMEM(q_weight.shape, bf16),
            pltpu.VMEM(key_matrix.shape, bf16),
            pltpu.VMEM(value_matrix.shape, bf16),
            pltpu.VMEM(q_gain.shape, f32),
            pltpu.VMEM(k_gain.shape, f32),
            pltpu.VMEM(o_weight.shape, bf16),
            pltpu.VMEM(freq.shape, f32),
            pltpu.VMEM(keys.shape, bf16),
            pltpu.VMEM(values.shape, bf16),
            pltpu.VMEM((nk, (heads + 2) * own, head_dim), f32),
            pltpu.VMEM((nk, (heads + 2) * own, head_dim), f32),
            pltpu.VMEM((nk, heads * own, head_dim), bf16),
            pltpu.VMEM((nk, heads * own, head_dim), bf16),
            pltpu.VMEM((nk, heads * own, head_dim), bf16),
            pltpu.VMEM((nk, 1, 128), f32),
            pltpu.VMEM((nk, 1, 128), f32),
            pltpu.VMEM((nk, heads * own, head_dim), bf16),
            pltpu.VMEM((nh, block, width), bf16),
            pltpu.VMEM((nh, block, width), bf16),
            dma((8,)),
        ]
        + [dma((nk,))] * 12
        + [dma((nh,))] * 2,
        compiler_params=pltpu.CompilerParams(
            collective_id=0, has_side_effects=True, vmem_limit_bytes=60 * 1024 * 1024
        ),
    )(
        tokens, q_weight, key_matrix, value_matrix, q_gain, k_gain, keys, values, o_weight,
        jnp.asarray(freq), lengths, positions,
    )


def solution(mesh):
    placed = (
        P(None, "kv"),
        P("kv", "head"),
        P("kv", "head"),
        P("kv", "head"),
        P("head", None),
        P("head", None),
        P(None, "kv", "head", None),
        P(None, "kv", "head", None),
        P(),
        P(),
        P("head", "kv"),
    )
    return jax.shard_map(
        functools.partial(on_device, mesh.shape["kv"], mesh.shape["head"]),
        mesh=mesh,
        in_specs=placed,
        out_specs=P("head", "kv"),
        check_vma=False,
    )
```

```python
import functools
import math

import jax
import jax.numpy as jnp
import numpy as np
from jax import lax
from jax.experimental import pallas as pl
from jax.experimental.pallas import tpu as pltpu
from jax.sharding import PartitionSpec as P

EPSILON = 1e-06
ROPE_BASE = 1000000.0
NEG = -1e30
MESH = pl.DeviceIdType.MESH


def column_to_row(col):
    rows = col.shape[0]
    wide = jnp.broadcast_to(col, (rows, 128))
    row_id = lax.broadcasted_iota(jnp.int32, (rows, 128), 0)
    lane_id = lax.broadcasted_iota(jnp.int32, (rows, 128), 1)
    return jnp.sum(jnp.where(row_id == lane_id, wide, 0.0), axis=0, keepdims=True)


def schedule(side):
    far = lambda at: sum(min(d, side - d) for d in at)
    spots = [(y, x) for y in range(side) for x in range(side)]
    ring = [[at for at in spots if far(at) == n] for n in range(side + 1)]
    batches = [
        ring[0] + ring[1][:-1],
        ring[2][:4],
        [at for n in range(side, 2, -1) for at in ring[n]],
        ring[2][4:] + ring[1][-1:],
    ]
    return [batch for batch in batches if batch]


def drain(ref, sem):
    pltpu.make_async_copy(ref, ref, sem).wait()


def kernel(
    nk, side, nh, drafts, batches,
    tokens, q_weight, key_matrix, value_matrix, q_gain, k_gain, keys, values, o_weight, freq,
    lengths_in, positions_in,
    out,
    tok_v, wq_v, wk_v, wv_v, qg_v, kg_v, wo_v, freq_v, keys_v, values_v, lengths, positions,
    part, part_in, query, attn, attn_in, lse, lse_in, attended, proj, proj_in,
    load_sem, key_sem, value_sem, query_rs, sems,
):
    (part_ss, part_rs, fresh_rs, query_ss, attn_ss, attn_rs, lse_ss, lse_rs, att_ss, att_rs,
     proj_ss, proj_rs) = [sems.at[n] for n in range(12)]
    me = lax.axis_index("kv")
    my_head = lax.axis_index("head")
    my_y, my_x = me // side, me % side
    reqs, local_len, head_dim = keys.shape
    rows = tokens.shape[1]
    heads = q_gain.shape[0]
    per = reqs // nk
    own = per * drafts
    group = heads * drafts
    scale = 1.0 / math.sqrt(head_dim)
    to_log2 = scale * math.log2(math.e)
    order = [at for batch in batches for at in batch]
    bounds = np.cumsum([0] + [len(batch) for batch in batches]).tolist()

    def ahead(n):
        y, x = order[n]
        return lax.rem(my_y + y, side) * side + lax.rem(my_x + x, side)

    def behind(n):
        y, x = order[n]
        return lax.rem(my_y + side - y, side) * side + lax.rem(my_x + side - x, side)

    def send(src, dst, send_sem, recv_sem, to):
        pltpu.make_async_remote_copy(
            src_ref=src, dst_ref=dst, send_sem=send_sem, recv_sem=recv_sem,
            device_id=to, device_id_type=MESH,
        ).start()

    barrier = pltpu.get_barrier_semaphore()
    for n in range(1, nk):
        pl.semaphore_signal(barrier, inc=1, device_id={"kv": ahead(n)}, device_id_type=MESH)
    for s in range(1, nh):
        pl.semaphore_signal(
            barrier, inc=1, device_id={"head": lax.rem(my_head + s, nh)}, device_id_type=MESH
        )

    loads = [
        pltpu.make_async_copy(src, dst, load_sem.at[n])
        for n, (src, dst) in enumerate(
            [
                (tokens, tok_v), (q_weight, wq_v), (key_matrix, wk_v), (value_matrix, wv_v),
                (q_gain, qg_v), (k_gain, kg_v), (freq, freq_v), (o_weight, wo_v),
                (lengths_in, lengths), (positions_in, positions),
            ]
        )
    ]
    for copy in loads:
        copy.start()
    for b in range(len(batches)):
        for n in range(bounds[b], bounds[b + 1]):
            at = pl.ds(per * behind(n), per)
            slot = pl.ds(per * n, per)
            pltpu.make_async_copy(keys.at[at], keys_v.at[slot], key_sem.at[b]).start()
            pltpu.make_async_copy(values.at[at], values_v.at[slot], value_sem.at[b]).start()

    for copy in loads[:4]:
        copy.wait()
    toks = tok_v[...].T

    def place_part(h, left):
        part[:, h * own : (h + 2) * own, :] = jnp.concatenate(
            [
                left[:, k * head_dim : (k + 1) * head_dim].reshape(nk, own, head_dim)
                for k in range(2)
            ],
            axis=1,
        )

    for h in range(0, heads, 2):
        weight = wq_v[:, h * head_dim : (h + 2) * head_dim]
        place_part(h, jnp.dot(toks, weight, preferred_element_type=jnp.float32))
    weight = jnp.concatenate([wk_v[...], wv_v[...]], axis=1)
    place_part(heads, jnp.dot(toks, weight, preferred_element_type=jnp.float32))

    pl.semaphore_wait(barrier, nk + nh - 2)

    q_rows = pl.ds(0, heads * own)
    kv_rows = pl.ds(heads * own, 2 * own)
    for some, sem in ((q_rows, part_rs), (kv_rows, fresh_rs)):
        for n in range(1, nk):
            send(
                part.at[ahead(n), some], part_in.at[n - 1, some], part_ss, sem,
                {"kv": ahead(n)},
            )

    for copy in loads[4:]:
        copy.wait()
    row_id = lax.broadcasted_iota(jnp.int32, (own, head_dim), 0)
    lane_id = lax.broadcasted_iota(jnp.int32, (own, head_dim), 1)
    place = [[positions[j, per * me + r] for j in range(drafts)] for r in range(per)]
    place_rows = jnp.zeros((own, head_dim), jnp.int32)
    for r in range(per):
        for j in range(drafts):
            place_rows = jnp.where(row_id == r * drafts + j, place[r][j], place_rows)
    angle = place_rows.astype(jnp.float32) * freq_v[...]
    cosine = jnp.cos(angle)
    sine = jnp.sin(angle)
    sine = jnp.where(lane_id < head_dim // 2, -sine, sine)
    fresh_row = lax.broadcasted_iota(jnp.int32, (per * group, 16), 0)
    fresh_col = lax.broadcasted_iota(jnp.int32, (per * group, 16), 1)
    seen = fresh_row < 0
    for r in range(per):
        for j in range(drafts):
            here = (fresh_row // group == r) & (fresh_row % drafts == j)
            for i in range(j + 1):
                hit = here & (fresh_col == r * drafts + i)
                if i < j:
                    hit = hit & (place[r][i] < place[r][j])
                seen = seen | hit

    def norm_rotate(vec, gain):
        vec = vec * lax.rsqrt(jnp.mean(vec * vec, axis=-1, keepdims=True) + EPSILON) * gain
        turned = pltpu.roll(vec.reshape(-1, head_dim), head_dim // 2, 1).reshape(vec.shape)
        return vec * cosine[None] + turned * sine[None]

    def gathered(some):
        raw = part[me, some]
        for n in range(nk - 1):
            raw = raw + part_in[n, some]
        return raw.reshape(-1, own, head_dim)

    drain(part_in.at[:, q_rows], part_rs)
    queries = norm_rotate(gathered(q_rows), qg_v[...][:, None, :])
    queries = jnp.swapaxes(queries.reshape(heads, per, drafts, head_dim), 0, 1)
    queries = queries.reshape(per * group, head_dim).astype(jnp.bfloat16)
    query[0] = queries
    for b in range(len(batches)):
        for n in range(max(bounds[b], 1), bounds[b + 1]):
            send(query.at[0], query.at[n], query_ss, query_rs.at[b], {"kv": ahead(n)})

    drain(part_in.at[:, kv_rows], fresh_rs)
    fresh_kv = gathered(kv_rows)
    fresh_k = norm_rotate(fresh_kv[:1], kg_v[...][:, None, :]).reshape(own, head_dim)
    pad = jnp.zeros((16 - own, head_dim), jnp.float32)
    fresh_k = jnp.concatenate([fresh_k, pad], axis=0).astype(jnp.bfloat16)
    fresh_v = jnp.concatenate([fresh_kv[1], pad], axis=0).astype(jnp.bfloat16)

    def softmax_part(scores, vals):
        top = jnp.max(scores, axis=-1, keepdims=True)
        weights = jnp.exp2((scores - top) * to_log2)
        total = jnp.sum(weights, axis=-1, keepdims=True)
        mixed = jnp.dot(weights.astype(jnp.bfloat16), vals, preferred_element_type=jnp.float32)
        return mixed / total, top * to_log2 + jnp.log2(total)

    def dot_t(left, right):
        return lax.dot_general(
            left, right, (((1,), (1,)), ((), ())), preferred_element_type=jnp.float32
        )

    fresh_out, fresh_lse = softmax_part(
        jnp.where(seen, dot_t(queries, fresh_k), NEG), fresh_v
    )
    fresh_lse = column_to_row(fresh_lse)

    spot = me * local_len + lax.broadcasted_iota(jnp.int32, (1, local_len), 1)
    zero = jnp.zeros((group, head_dim), jnp.bfloat16)

    def rows_of(array, r):
        return array[r * group : (r + 1) * group]

    def attend(n):
        block = query[n]
        wide = jnp.concatenate(
            [
                jnp.concatenate(
                    [rows_of(block, r) if c == r else zero for c in range(per)], axis=1
                )
                for r in range(per)
            ],
            axis=0,
        )
        ks = jnp.concatenate([keys_v[per * n + r] for r in range(per)], axis=1)
        vs = jnp.concatenate([values_v[per * n + r] for r in range(per)], axis=1)
        scores = dot_t(wide, ks)
        scores = jnp.concatenate(
            [
                jnp.where(spot < lengths[per * behind(n) + r], rows_of(scores, r), NEG)
                for r in range(per)
            ],
            axis=0,
        )
        mixed, stat = softmax_part(scores, vs)
        mixed = jnp.concatenate(
            [rows_of(mixed, r)[:, r * head_dim : (r + 1) * head_dim] for r in range(per)], axis=0
        )
        return mixed, stat

    for b in range(len(batches)):
        slots = range(bounds[b], bounds[b + 1])
        away = range(max(bounds[b], 1), bounds[b + 1])
        drain(query.at[pl.ds(away[0], len(away))], query_rs.at[b])
        block = pl.ds(per * slots[0], per * len(slots))
        drain(keys_v.at[block], key_sem.at[b])
        drain(values_v.at[block], value_sem.at[b])
        results = [attend(n) for n in slots]
        for n, (mixed, stat) in zip(slots, results):
            attn[n] = mixed.astype(jnp.bfloat16)
            lse[n] = column_to_row(stat)
        for n in away:
            send(attn.at[n], attn_in.at[n - 1], attn_ss, attn_rs, {"kv": behind(n)})
            send(lse.at[n], lse_in.at[n - 1], lse_ss, lse_rs, {"kv": behind(n)})

    drain(lse_in, lse_rs)
    stats = jnp.concatenate([lse[0], fresh_lse] + [lse_in[n] for n in range(nk - 1)], axis=0)
    ratio = jnp.exp2(stats - jnp.max(stats, axis=0, keepdims=True))
    ratio = ratio / jnp.sum(ratio, axis=0, keepdims=True)
    ratio = jnp.concatenate([ratio, jnp.zeros((128 - nk - 1, 128), jnp.float32)], axis=0).T
    ratio = ratio[: per * group]
    merged = attn[0].astype(jnp.float32) * ratio[:, 0:1] + fresh_out * ratio[:, 1:2]
    drain(attn_in, attn_rs)
    for n in range(nk - 1):
        merged = merged + attn_in[n].astype(jnp.float32) * ratio[:, n + 2 : n + 3]
    merged = jnp.swapaxes(merged.reshape(per, heads, drafts, head_dim), 0, 1)
    attended[me] = merged.reshape(heads * own, head_dim).astype(jnp.bfloat16)
    for n in range(1, nk):
        send(attended.at[me], attended.at[me], att_ss, att_rs, {"kv": ahead(n)})
    drain(attended.at[pl.ds(0, nk - 1)], att_rs)

    total = None
    for h in range(0, heads, 2):
        pair = attended[:, h * own : (h + 2) * own, :].astype(jnp.float32)
        pair = pair.reshape(nk, 2, own, head_dim)
        for k in range(2):
            side_in = pair[:, k].reshape(rows, head_dim).astype(jnp.bfloat16)
            term = dot_t(side_in, wo_v[:, (h + k) * head_dim : (h + k + 1) * head_dim])
            total = term if total is None else total + term
    proj[...] = total.astype(jnp.bfloat16).reshape(proj.shape)
    for s in range(1, nh):
        target = lax.rem(my_head + s, nh)
        send(proj.at[target], proj_in.at[s - 1], proj_ss, proj_rs, {"head": target})
    drain(proj_in, proj_rs)
    result = proj[my_head].astype(jnp.float32)
    for s in range(nh - 1):
        result = result + proj_in[s].astype(jnp.float32)
    out[...] = result.astype(jnp.bfloat16)

    drain(part_in, part_ss)
    drain(attn_in, query_ss)
    drain(attn_in, attn_ss)
    drain(lse_in, lse_ss)
    drain(attn_in, att_ss)
    drain(proj_in, proj_ss)


def on_device(
    nk, nh,
    tokens, q_weight, key_matrix, value_matrix, q_gain, k_gain, keys, values, lengths, positions,
    o_weight,
):
    rows = tokens.shape[0]
    reqs, drafts = positions.shape
    width = o_weight.shape[1]
    tokens, o_weight, positions = tokens.T, o_weight.T, positions.T
    _, local_len, _, head_dim = keys.shape
    keys = keys.reshape(reqs, local_len, head_dim)
    values = values.reshape(reqs, local_len, head_dim)
    heads = q_gain.shape[0]
    side = math.isqrt(nk)
    batches = schedule(side)
    own = rows // nk
    block = rows // nh
    exponent = np.arange(head_dim // 2, dtype=np.float64) * 2.0 / head_dim
    freq = np.tile((ROPE_BASE ** -exponent).astype(np.float32), 2)[None]
    bf16, f32 = jnp.bfloat16, jnp.float32
    dma = pltpu.SemaphoreType.DMA
    hbm = pl.BlockSpec(memory_space=pltpu.HBM)
    return pl.pallas_call(
        functools.partial(kernel, nk, side, nh, drafts, batches),
        out_shape=jax.ShapeDtypeStruct((block, width), bf16),
        in_specs=[hbm] * 12,
        out_specs=pl.BlockSpec(memory_space=pltpu.VMEM),
        scratch_shapes=[
            pltpu.VMEM(tokens.shape, bf16),
            pltpu.VMEM(q_weight.shape, bf16),
            pltpu.VMEM(key_matrix.shape, bf16),
            pltpu.VMEM(value_matrix.shape, bf16),
            pltpu.VMEM(q_gain.shape, f32),
            pltpu.VMEM(k_gain.shape, f32),
            pltpu.VMEM(o_weight.shape, bf16),
            pltpu.VMEM(freq.shape, f32),
            pltpu.VMEM(keys.shape, bf16),
            pltpu.VMEM(values.shape, bf16),
            pltpu.SMEM(lengths.shape, jnp.int32),
            pltpu.SMEM(positions.shape, jnp.int32),
            pltpu.VMEM((nk, (heads + 2) * own, head_dim), f32),
            pltpu.VMEM((nk - 1, (heads + 2) * own, head_dim), f32),
            pltpu.VMEM((nk, heads * own, head_dim), bf16),
            pltpu.VMEM((nk, heads * own, head_dim), bf16),
            pltpu.VMEM((nk - 1, heads * own, head_dim), bf16),
            pltpu.VMEM((nk, 1, 128), f32),
            pltpu.VMEM((nk - 1, 1, 128), f32),
            pltpu.VMEM((nk, heads * own, head_dim), bf16),
            pltpu.VMEM((nh, block, width), bf16),
            pltpu.VMEM((nh - 1, block, width), bf16),
            dma((10,)),
            dma((len(batches),)),
            dma((len(batches),)),
            dma((len(batches),)),
            dma((12,)),
        ],
        compiler_params=pltpu.CompilerParams(
            collective_id=0, has_side_effects=True, vmem_limit_bytes=60 * 1024 * 1024
        ),
    )(
        tokens, q_weight, key_matrix, value_matrix, q_gain, k_gain, keys, values, o_weight,
        jnp.asarray(freq), lengths, positions,
    )


def solution(mesh):
    placed = (
        P(None, "kv"),
        P("kv", "head"),
        P("kv", "head"),
        P("kv", "head"),
        P("head", None),
        P("head", None),
        P(None, "kv", "head", None),
        P(None, "kv", "head", None),
        P(),
        P(),
        P("head", "kv"),
    )
    return jax.shard_map(
        functools.partial(on_device, mesh.shape["kv"], mesh.shape["head"]),
        mesh=mesh,
        in_specs=placed,
        out_specs=P("head", "kv"),
        check_vma=False,
    )
```

```python
import functools
import math

import jax
import jax.numpy as jnp
import numpy as np
from jax import lax
from jax.experimental import pallas as pl
from jax.experimental.pallas import tpu as pltpu
from jax.sharding import PartitionSpec as P

EPSILON = 1e-06
ROPE_BASE = 1000000.0
NEG = -1e30
MESH = pl.DeviceIdType.MESH


def column_to_row(col, first):
    rows = col.shape[0]
    wide = jnp.broadcast_to(col, (rows, 128))
    row_id = lax.broadcasted_iota(jnp.int32, (rows, 128), 0)
    lane_id = lax.broadcasted_iota(jnp.int32, (rows, 128), 1)
    return jnp.sum(jnp.where(row_id + first == lane_id, wide, 0.0), axis=0, keepdims=True)


def by_distance(side):
    spots = [(y, x) for y in range(side) for x in range(side)]
    return sorted(spots, key=lambda at: sum(min(d, side - d) for d in at))


def drain(ref, sem):
    pltpu.make_async_copy(ref, ref, sem).wait()


def kernel(
    nk, side, nh, drafts,
    tokens, q_weight, key_matrix, value_matrix, q_gain, k_gain, keys, values, o_weight, freq,
    lengths_in, positions_in,
    out,
    tok_v, wq_v, wk_v, wv_v, qg_v, kg_v, wo_v, freq_v, keys_v, values_v, lengths, positions,
    part, part_in, fresh, fresh_in, query, attn, attn_in, lse, lse_in, attended, proj, proj_in,
    load_sem, key_sem, value_sem, part_rs, query_rs, sems,
):
    (part_ss, fresh_ss, fresh_rs, query_ss, attn_ss, attn_rs, lse_ss, lse_rs, att_ss, att_rs,
     proj_ss, proj_rs) = [sems.at[n] for n in range(12)]
    me = lax.axis_index("kv")
    my_head = lax.axis_index("head")
    my_y, my_x = me // side, me % side
    reqs, local_len, head_dim = keys.shape
    rows = tokens.shape[1]
    heads = q_gain.shape[0]
    per = reqs // nk
    own = per * drafts
    group = heads * drafts
    scale = 1.0 / math.sqrt(head_dim)
    to_log2 = scale * math.log2(math.e)
    order = by_distance(side)
    half = nk // 2

    def ahead(n):
        y, x = order[n]
        return lax.rem(my_y + y, side) * side + lax.rem(my_x + x, side)

    def behind(n):
        y, x = order[n]
        return lax.rem(my_y + side - y, side) * side + lax.rem(my_x + side - x, side)

    def send(src, dst, send_sem, recv_sem, to):
        pltpu.make_async_remote_copy(
            src_ref=src, dst_ref=dst, send_sem=send_sem, recv_sem=recv_sem,
            device_id=to, device_id_type=MESH,
        ).start()

    barrier = pltpu.get_barrier_semaphore()
    for n in reversed(range(1, nk)):
        pl.semaphore_signal(barrier, inc=1, device_id={"kv": ahead(n)}, device_id_type=MESH)
    for s in range(1, nh):
        pl.semaphore_signal(
            barrier, inc=1, device_id={"head": lax.rem(my_head + s, nh)}, device_id_type=MESH
        )

    loads = [
        pltpu.make_async_copy(src, dst, load_sem.at[n])
        for n, (src, dst) in enumerate(
            [
                (tokens, tok_v), (q_weight, wq_v), (key_matrix, wk_v), (value_matrix, wv_v),
                (q_gain, qg_v), (k_gain, kg_v), (freq, freq_v), (o_weight, wo_v),
                (lengths_in, lengths), (positions_in, positions),
            ]
        )
    ]
    for copy in loads[:4]:
        copy.start()
    for copy in loads[:4]:
        copy.wait()
    toks = tok_v[...].T

    upper = lax.broadcasted_iota(jnp.int32, (rows, head_dim), 0) % own < drafts

    def split(first, second):
        low = jnp.where(upper, first, pltpu.roll(second, drafts, 0))
        high = jnp.where(upper, pltpu.roll(first, rows - drafts, 0), second)
        return [low.reshape(nk, own, head_dim), high.reshape(nk, own, head_dim)]

    for h in range(0, heads, 2):
        weight = wq_v[:, h * head_dim : (h + 2) * head_dim]
        both = jnp.dot(toks, weight, preferred_element_type=jnp.float32)
        for r, piece in enumerate(split(both[:, :head_dim], both[:, head_dim:])):
            part[r, :, h * drafts : (h + 2) * drafts, :] = piece
    weight = jnp.concatenate([wk_v[...], wv_v[...]], axis=1)
    both = jnp.dot(toks, weight, preferred_element_type=jnp.float32)
    fresh[...] = jnp.concatenate(
        [both[:, k * head_dim : (k + 1) * head_dim].reshape(nk, own, head_dim) for k in range(2)],
        axis=1,
    )

    pl.semaphore_wait(barrier, nk + nh - 2)

    for r in range(per):
        for n in range(1, nk):
            send(
                part.at[r, ahead(n)], part_in.at[r, n - 1], part_ss, part_rs.at[r],
                {"kv": ahead(n)},
            )
    for n in range(1, nk):
        send(fresh.at[ahead(n)], fresh_in.at[n - 1], fresh_ss, fresh_rs, {"kv": ahead(n)})

    for copy in loads[4:]:
        copy.start()
    for r in range(per):
        for b in ((0, 1), (1, 0))[r]:
            for n in range(b * half, (b + 1) * half):
                at = per * behind(n) + r
                pltpu.make_async_copy(
                    keys.at[at], keys_v.at[r * nk + n], key_sem.at[2 * r + b]
                ).start()
                pltpu.make_async_copy(
                    values.at[at], values_v.at[r * nk + n], value_sem.at[2 * r + b]
                ).start()
    for copy in loads[4:]:
        copy.wait()
    row_id = lax.broadcasted_iota(jnp.int32, (own, head_dim), 0)
    lane_id = lax.broadcasted_iota(jnp.int32, (own, head_dim), 1)
    place = [[positions[j, per * me + r] for j in range(drafts)] for r in range(per)]
    place_rows = jnp.zeros((own, head_dim), jnp.int32)
    for r in range(per):
        for j in range(drafts):
            place_rows = jnp.where(row_id == r * drafts + j, place[r][j], place_rows)
    angle = place_rows.astype(jnp.float32) * freq_v[...]
    cosine = jnp.cos(angle)
    sine = jnp.sin(angle)
    sine = jnp.where(lane_id < head_dim // 2, -sine, sine)
    fresh_row = lax.broadcasted_iota(jnp.int32, (per * group, 16), 0)
    fresh_col = lax.broadcasted_iota(jnp.int32, (per * group, 16), 1)
    seen = fresh_row < 0
    for r in range(per):
        for j in range(drafts):
            here = (fresh_row // group == r) & (fresh_row % drafts == j)
            for i in range(j + 1):
                hit = here & (fresh_col == r * drafts + i)
                if i < j:
                    hit = hit & (place[r][i] < place[r][j])
                seen = seen | hit

    top_half = row_id < drafts

    def spread(array, r):
        turned = pltpu.roll(array, drafts, 0)
        return jnp.where(top_half, array, turned) if r == 0 else jnp.where(top_half, turned, array)

    turns = [(spread(cosine, r)[None], spread(sine, r)[None]) for r in range(per)]
    gains = qg_v[...]
    gains = jnp.concatenate(
        [
            jnp.where(top_half, gains[h : h + 1], gains[h + 1 : h + 2])[None]
            for h in range(0, heads, 2)
        ],
        axis=0,
    )

    def norm_rotate(vec, gain, turn):
        vec = vec * lax.rsqrt(jnp.mean(vec * vec, axis=-1, keepdims=True) + EPSILON) * gain
        turned = pltpu.roll(vec.reshape(-1, head_dim), head_dim // 2, 1).reshape(vec.shape)
        return vec * turn[0] + turned * turn[1]

    queries = []
    for r in range(per):
        drain(part_in.at[r], part_rs.at[r])
        raw = part[r, me]
        for n in range(nk - 1):
            raw = raw + part_in[r, n]
        mine = norm_rotate(raw.reshape(heads // 2, own, head_dim), gains, turns[r])
        mine = mine.reshape(group, head_dim).astype(jnp.bfloat16)
        queries.append(mine)
        query[r, 0] = mine
        for b in ((0, 1), (1, 0))[r]:
            for n in range(max(b * half, 1), (b + 1) * half):
                send(
                    query.at[r, 0], query.at[r, n], query_ss, query_rs.at[2 * r + b],
                    {"kv": ahead(n)},
                )
    queries = jnp.concatenate(queries, axis=0)

    drain(fresh_in, fresh_rs)
    fresh_kv = fresh[me]
    for n in range(nk - 1):
        fresh_kv = fresh_kv + fresh_in[n]
    fresh_k = norm_rotate(fresh_kv[:own][None], kg_v[...], (cosine[None], sine[None]))
    pad = jnp.zeros((16 - own, head_dim), jnp.float32)
    fresh_k = jnp.concatenate([fresh_k.reshape(own, head_dim), pad], axis=0).astype(jnp.bfloat16)
    fresh_v = jnp.concatenate([fresh_kv[own:], pad], axis=0).astype(jnp.bfloat16)

    def softmax_part(scores, vals):
        top = jnp.max(scores, axis=-1, keepdims=True)
        weights = jnp.exp2((scores - top) * to_log2)
        total = jnp.sum(weights, axis=-1, keepdims=True)
        mixed = jnp.dot(weights.astype(jnp.bfloat16), vals, preferred_element_type=jnp.float32)
        return mixed / total, top * to_log2 + jnp.log2(total)

    def dot_t(left, right):
        return lax.dot_general(
            left, right, (((1,), (1,)), ((), ())), preferred_element_type=jnp.float32
        )

    fresh_out, fresh_lse = softmax_part(
        jnp.where(seen, dot_t(queries, fresh_k), NEG), fresh_v
    )
    fresh_lse = column_to_row(fresh_lse, 0)

    spot = me * local_len + lax.broadcasted_iota(jnp.int32, (1, local_len), 1)
    zero = jnp.zeros((group, head_dim), jnp.bfloat16)

    def rows_of(array, r):
        return array[r * group : (r + 1) * group]

    def attend(r, n):
        wide = jnp.concatenate(
            [
                jnp.concatenate([query[r, n], zero], axis=1),
                jnp.concatenate([zero, query[r, n + 1]], axis=1),
            ],
            axis=0,
        )
        at = r * nk + n
        scores = dot_t(wide, jnp.concatenate([keys_v[at], keys_v[at + 1]], axis=1))
        scores = jnp.concatenate(
            [
                jnp.where(spot < lengths[per * behind(n + k) + r], rows_of(scores, k), NEG)
                for k in range(2)
            ],
            axis=0,
        )
        mixed, stat = softmax_part(
            scores, jnp.concatenate([values_v[at], values_v[at + 1]], axis=1)
        )
        return [
            (rows_of(mixed, k)[:, k * head_dim : (k + 1) * head_dim], rows_of(stat, k))
            for k in range(2)
        ]

    for r in range(per):
        for b in ((0, 1), (1, 0))[r]:
            slots = range(b * half, (b + 1) * half)
            away = slots[1:] if b == 0 else slots
            drain(query.at[r, pl.ds(away[0], len(away))], query_rs.at[2 * r + b])
            block = pl.ds(r * nk + b * half, half)
            drain(keys_v.at[block], key_sem.at[2 * r + b])
            drain(values_v.at[block], value_sem.at[2 * r + b])
            results = [part_of for n in slots[::2] for part_of in attend(r, n)]
            for n, (mixed, stat) in zip(slots, results):
                attn[r, n] = mixed.astype(jnp.bfloat16)
                if r == 0:
                    lse[n] = column_to_row(stat, 0)
                else:
                    lse[n] = lse[n] + column_to_row(stat, group)
            for n in away:
                send(attn.at[r, n], attn_in.at[r, n - 1], attn_ss, attn_rs, {"kv": behind(n)})
                if r == per - 1:
                    send(lse.at[n], lse_in.at[n - 1], lse_ss, lse_rs, {"kv": behind(n)})

    drain(lse_in, lse_rs)
    stats = jnp.concatenate([lse[0], fresh_lse] + [lse_in[n] for n in range(nk - 1)], axis=0)
    ratio = jnp.exp2(stats - jnp.max(stats, axis=0, keepdims=True))
    ratio = ratio / jnp.sum(ratio, axis=0, keepdims=True)
    ratio = jnp.concatenate([ratio, jnp.zeros((128 - nk - 1, 128), jnp.float32)], axis=0).T
    ratio = ratio[: per * group]
    merged = attn[:, 0].astype(jnp.float32).reshape(per * group, head_dim) * ratio[:, 0:1] + fresh_out * ratio[:, 1:2]
    drain(attn_in, attn_rs)
    for n in range(nk - 1):
        piece = attn_in[:, n].astype(jnp.float32).reshape(per * group, head_dim)
        merged = merged + piece * ratio[:, n + 2 : n + 3]
    merged = jnp.swapaxes(merged.reshape(per, heads, drafts, head_dim), 0, 1)
    merged = merged.reshape(heads, own, head_dim)
    attended[me] = jnp.concatenate(
        [
            jnp.concatenate([merged[h + k * heads // 2] for h in range(heads // 2)], axis=1)
            for k in range(2)
        ],
        axis=0,
    ).astype(jnp.bfloat16)
    for n in range(1, nk):
        send(attended.at[me], attended.at[me], att_ss, att_rs, {"kv": ahead(n)})
    drain(attended.at[pl.ds(0, nk - 1)], att_rs)

    everyone = attended[...].reshape(nk * 2 * own, heads * head_dim // 2)
    total = None
    for k in range(2):
        half = pl.ds(k * heads * head_dim // 2, heads * head_dim // 2)
        term = dot_t(everyone, wo_v[:, half]).reshape(nk, 2, own, -1)[:, k]
        total = term if total is None else total + term
    width = out.shape[1]
    spare = jnp.zeros((rows, proj.shape[2] - width), jnp.float32)
    total = jnp.concatenate([total.reshape(rows, width), spare], axis=1)
    proj[...] = total.astype(jnp.bfloat16).reshape(proj.shape)
    for s in range(1, nh):
        target = lax.rem(my_head + s, nh)
        send(proj.at[target], proj_in.at[s - 1], proj_ss, proj_rs, {"head": target})
    drain(proj_in, proj_rs)
    result = proj[my_head].astype(jnp.float32)
    for s in range(nh - 1):
        result = result + proj_in[s].astype(jnp.float32)
    out[...] = result[:, :width].astype(jnp.bfloat16)

    drain(part_in, part_ss)
    drain(fresh_in, fresh_ss)
    drain(attn_in, query_ss)
    drain(attn_in, attn_ss)
    drain(lse_in, lse_ss)
    drain(attended.at[pl.ds(0, nk - 1)], att_ss)
    drain(proj_in, proj_ss)


def on_device(
    nk, nh,
    tokens, q_weight, key_matrix, value_matrix, q_gain, k_gain, keys, values, lengths, positions,
    o_weight,
):
    rows = tokens.shape[0]
    reqs, drafts = positions.shape
    width = o_weight.shape[1]
    tokens, o_weight, positions = tokens.T, o_weight.T, positions.T
    _, local_len, _, head_dim = keys.shape
    keys = keys.reshape(reqs, local_len, head_dim)
    values = values.reshape(reqs, local_len, head_dim)
    heads = q_gain.shape[0]
    side = math.isqrt(nk)
    own = rows // nk
    per = reqs // nk
    group = heads * drafts
    block = rows // nh
    padded = -(-width // 128) * 128
    exponent = np.arange(head_dim // 2, dtype=np.float64) * 2.0 / head_dim
    freq = np.tile((ROPE_BASE ** -exponent).astype(np.float32), 2)[None]
    bf16, f32 = jnp.bfloat16, jnp.float32
    dma = pltpu.SemaphoreType.DMA
    hbm = pl.BlockSpec(memory_space=pltpu.HBM)
    return pl.pallas_call(
        functools.partial(kernel, nk, side, nh, drafts),
        out_shape=jax.ShapeDtypeStruct((block, width), bf16),
        in_specs=[hbm] * 12,
        out_specs=pl.BlockSpec(memory_space=pltpu.VMEM),
        scratch_shapes=[
            pltpu.VMEM(tokens.shape, bf16),
            pltpu.VMEM(q_weight.shape, bf16),
            pltpu.VMEM(key_matrix.shape, bf16),
            pltpu.VMEM(value_matrix.shape, bf16),
            pltpu.VMEM(q_gain.shape, f32),
            pltpu.VMEM(k_gain.shape, f32),
            pltpu.VMEM(o_weight.shape, bf16),
            pltpu.VMEM(freq.shape, f32),
            pltpu.VMEM(keys.shape, bf16),
            pltpu.VMEM(values.shape, bf16),
            pltpu.SMEM(lengths.shape, jnp.int32),
            pltpu.SMEM(positions.shape, jnp.int32),
            pltpu.VMEM((per, nk, group, head_dim), f32),
            pltpu.VMEM((per, nk - 1, group, head_dim), f32),
            pltpu.VMEM((nk, 2 * own, head_dim), f32),
            pltpu.VMEM((nk - 1, 2 * own, head_dim), f32),
            pltpu.VMEM((per, nk, group, head_dim), bf16),
            pltpu.VMEM((per, nk, group, head_dim), bf16),
            pltpu.VMEM((per, nk - 1, group, head_dim), bf16),
            pltpu.VMEM((nk, 1, 128), f32),
            pltpu.VMEM((nk - 1, 1, 128), f32),
            pltpu.VMEM((nk, 2 * own, heads * head_dim // 2), bf16),
            pltpu.VMEM((nh, block, padded), bf16),
            pltpu.VMEM((nh - 1, block, padded), bf16),
            dma((10,)),
            dma((2 * per,)),
            dma((2 * per,)),
            dma((per,)),
            dma((2 * per,)),
            dma((12,)),
        ],
        compiler_params=pltpu.CompilerParams(
            collective_id=0, has_side_effects=True, vmem_limit_bytes=60 * 1024 * 1024
        ),
    )(
        tokens, q_weight, key_matrix, value_matrix, q_gain, k_gain, keys, values, o_weight,
        jnp.asarray(freq), lengths, positions,
    )


def solution(mesh):
    placed = (
        P(None, "kv"),
        P("kv", "head"),
        P("kv", "head"),
        P("kv", "head"),
        P("head", None),
        P("head", None),
        P(None, "kv", "head", None),
        P(None, "kv", "head", None),
        P(),
        P(),
        P("head", "kv"),
    )
    return jax.shard_map(
        functools.partial(on_device, mesh.shape["kv"], mesh.shape["head"]),
        mesh=mesh,
        in_specs=placed,
        out_specs=P("head", "kv"),
        check_vma=False,
    )
```

```python
import functools
import math

import jax
import jax.numpy as jnp
import numpy as np
from jax import lax
from jax.experimental import pallas as pl
from jax.experimental.pallas import tpu as pltpu
from jax.sharding import PartitionSpec as P

EPSILON = 1e-06
ROPE_BASE = 1000000.0
NEG = -1e30
MESH = pl.DeviceIdType.MESH


def column_to_row(col, first):
    rows = col.shape[0]
    wide = jnp.broadcast_to(col, (rows, 128))
    row_id = lax.broadcasted_iota(jnp.int32, (rows, 128), 0)
    lane_id = lax.broadcasted_iota(jnp.int32, (rows, 128), 1)
    return jnp.sum(jnp.where(row_id + first == lane_id, wide, 0.0), axis=0, keepdims=True)


def by_distance(side):
    spots = [(y, x) for y in range(side) for x in range(side)]
    return sorted(spots, key=lambda at: sum(min(d, side - d) for d in at))


def drain(ref, sem):
    pltpu.make_async_copy(ref, ref, sem).wait()


def kernel(
    nk, side, nh, drafts,
    tokens, q_weight, key_matrix, value_matrix, q_gain, k_gain, keys, values, o_weight, freq,
    lengths_in, positions_in,
    out,
    tok_v, wq_v, wk_v, wv_v, qg_v, kg_v, wo_v, freq_v, keys_v, values_v, lengths, positions,
    part, part_in, fresh, fresh_in, query, attn, attn_in, lse, lse_in, attended, proj, proj_in,
    load_sem, key_sem, value_sem, part_rs, query_rs, sems,
):
    (part_ss, fresh_ss, fresh_rs, query_ss, attn_ss, attn_rs, lse_ss, lse_rs, att_ss, att_rs,
     proj_ss, proj_rs) = [sems.at[n] for n in range(12)]
    me = lax.axis_index("kv")
    my_head = lax.axis_index("head")
    my_y, my_x = me // side, me % side
    reqs, local_len, head_dim = keys.shape
    rows = tokens.shape[1]
    heads = q_gain.shape[0]
    per = reqs // nk
    own = per * drafts
    group = heads * drafts
    scale = 1.0 / math.sqrt(head_dim)
    to_log2 = scale * math.log2(math.e)
    order = by_distance(side)
    quarter = max(nk // 4, 2)
    spans = [(0, quarter), (quarter, 2 * quarter), (2 * quarter, nk)]
    spans = [span for span in spans if span[0] < span[1]]
    stages = [spans, spans[::-1]]
    steps = len(stages[0])

    def ahead(n):
        y, x = order[n]
        return lax.rem(my_y + y, side) * side + lax.rem(my_x + x, side)

    def behind(n):
        y, x = order[n]
        return lax.rem(my_y + side - y, side) * side + lax.rem(my_x + side - x, side)

    def send(src, dst, send_sem, recv_sem, to):
        pltpu.make_async_remote_copy(
            src_ref=src, dst_ref=dst, send_sem=send_sem, recv_sem=recv_sem,
            device_id=to, device_id_type=MESH,
        ).start()

    barrier = pltpu.get_barrier_semaphore()
    for n in reversed(range(1, nk)):
        pl.semaphore_signal(barrier, inc=1, device_id={"kv": ahead(n)}, device_id_type=MESH)
    for s in range(1, nh):
        pl.semaphore_signal(
            barrier, inc=1, device_id={"head": lax.rem(my_head + s, nh)}, device_id_type=MESH
        )

    loads = [
        pltpu.make_async_copy(src, dst, load_sem.at[n])
        for n, (src, dst) in enumerate(
            [
                (tokens, tok_v), (q_weight, wq_v), (key_matrix, wk_v), (value_matrix, wv_v),
                (q_gain, qg_v), (k_gain, kg_v), (freq, freq_v), (o_weight, wo_v),
                (lengths_in, lengths), (positions_in, positions),
            ]
        )
    ]
    for copy in loads[:4]:
        copy.start()
    for copy in loads[:4]:
        copy.wait()
    toks = tok_v[...].T

    upper = lax.broadcasted_iota(jnp.int32, (rows, head_dim), 0) % own < drafts

    def split(first, second):
        low = jnp.where(upper, first, pltpu.roll(second, drafts, 0))
        high = jnp.where(upper, pltpu.roll(first, rows - drafts, 0), second)
        return [low.reshape(nk, own, head_dim), high.reshape(nk, own, head_dim)]

    for h in range(0, heads, 2):
        weight = wq_v[:, h * head_dim : (h + 2) * head_dim]
        both = jnp.dot(toks, weight, preferred_element_type=jnp.float32)
        for r, piece in enumerate(split(both[:, :head_dim], both[:, head_dim:])):
            part[r, :, h * drafts : (h + 2) * drafts, :] = piece
    weight = jnp.concatenate([wk_v[...], wv_v[...]], axis=1)
    both = jnp.dot(toks, weight, preferred_element_type=jnp.float32)
    fresh[...] = jnp.concatenate(
        [both[:, k * head_dim : (k + 1) * head_dim].reshape(nk, own, head_dim) for k in range(2)],
        axis=1,
    )

    pl.semaphore_wait(barrier, nk + nh - 2)

    for r in range(per):
        for n in range(1, nk):
            send(
                part.at[r, ahead(n)], part_in.at[r, n - 1], part_ss, part_rs.at[r],
                {"kv": ahead(n)},
            )
    for n in range(1, nk):
        send(fresh.at[ahead(n)], fresh_in.at[n - 1], fresh_ss, fresh_rs, {"kv": ahead(n)})

    for copy in loads[4:]:
        copy.start()
    for r in range(per):
        for b, (low, high) in enumerate(stages[r]):
            for n in range(low, high):
                at = per * behind(n) + r
                pltpu.make_async_copy(
                    keys.at[at], keys_v.at[r * nk + n], key_sem.at[steps * r + b]
                ).start()
                pltpu.make_async_copy(
                    values.at[at], values_v.at[r * nk + n], value_sem.at[steps * r + b]
                ).start()
    for copy in loads[4:]:
        copy.wait()
    row_id = lax.broadcasted_iota(jnp.int32, (own, head_dim), 0)
    lane_id = lax.broadcasted_iota(jnp.int32, (own, head_dim), 1)
    place = [[positions[j, per * me + r] for j in range(drafts)] for r in range(per)]
    place_rows = jnp.zeros((own, head_dim), jnp.int32)
    for r in range(per):
        for j in range(drafts):
            place_rows = jnp.where(row_id == r * drafts + j, place[r][j], place_rows)
    angle = place_rows.astype(jnp.float32) * freq_v[...]
    cosine = jnp.cos(angle)
    sine = jnp.sin(angle)
    sine = jnp.where(lane_id < head_dim // 2, -sine, sine)
    fresh_row = lax.broadcasted_iota(jnp.int32, (per * group, 16), 0)
    fresh_col = lax.broadcasted_iota(jnp.int32, (per * group, 16), 1)
    seen = fresh_row < 0
    for r in range(per):
        for j in range(drafts):
            here = (fresh_row // group == r) & (fresh_row % drafts == j)
            for i in range(j + 1):
                hit = here & (fresh_col == r * drafts + i)
                if i < j:
                    hit = hit & (place[r][i] < place[r][j])
                seen = seen | hit

    top_half = row_id < drafts

    def spread(array, r):
        turned = pltpu.roll(array, drafts, 0)
        return jnp.where(top_half, array, turned) if r == 0 else jnp.where(top_half, turned, array)

    turns = [(spread(cosine, r)[None], spread(sine, r)[None]) for r in range(per)]
    gains = qg_v[...]
    gains = jnp.concatenate(
        [
            jnp.where(top_half, gains[h : h + 1], gains[h + 1 : h + 2])[None]
            for h in range(0, heads, 2)
        ],
        axis=0,
    )

    def norm_rotate(vec, gain, turn):
        vec = vec * lax.rsqrt(jnp.mean(vec * vec, axis=-1, keepdims=True) + EPSILON) * gain
        turned = pltpu.roll(vec.reshape(-1, head_dim), head_dim // 2, 1).reshape(vec.shape)
        return vec * turn[0] + turned * turn[1]

    queries = []
    for r in range(per):
        drain(part_in.at[r], part_rs.at[r])
        raw = part[r, me]
        for n in range(nk - 1):
            raw = raw + part_in[r, n]
        mine = norm_rotate(raw.reshape(heads // 2, own, head_dim), gains, turns[r])
        mine = mine.reshape(group, head_dim).astype(jnp.bfloat16)
        queries.append(mine)
        query[r, 0] = mine
        for b, (low, high) in enumerate(stages[r]):
            for n in range(max(low, 1), high):
                send(
                    query.at[r, 0], query.at[r, n], query_ss, query_rs.at[steps * r + b],
                    {"kv": ahead(n)},
                )
    queries = jnp.concatenate(queries, axis=0)

    drain(fresh_in, fresh_rs)
    fresh_kv = fresh[me]
    for n in range(nk - 1):
        fresh_kv = fresh_kv + fresh_in[n]
    fresh_k = norm_rotate(fresh_kv[:own][None], kg_v[...], (cosine[None], sine[None]))
    pad = jnp.zeros((16 - own, head_dim), jnp.float32)
    fresh_k = jnp.concatenate([fresh_k.reshape(own, head_dim), pad], axis=0).astype(jnp.bfloat16)
    fresh_v = jnp.concatenate([fresh_kv[own:], pad], axis=0).astype(jnp.bfloat16)

    def softmax_part(scores, vals):
        top = jnp.max(scores, axis=-1, keepdims=True)
        weights = jnp.exp2((scores - top) * to_log2)
        total = jnp.sum(weights, axis=-1, keepdims=True)
        mixed = jnp.dot(weights.astype(jnp.bfloat16), vals, preferred_element_type=jnp.float32)
        return mixed / total, top * to_log2 + jnp.log2(total)

    def dot_t(left, right):
        return lax.dot_general(
            left, right, (((1,), (1,)), ((), ())), preferred_element_type=jnp.float32
        )

    fresh_out, fresh_lse = softmax_part(
        jnp.where(seen, dot_t(queries, fresh_k), NEG), fresh_v
    )
    fresh_lse = column_to_row(fresh_lse, 0)

    spot = me * local_len + lax.broadcasted_iota(jnp.int32, (1, local_len), 1)
    zero = jnp.zeros((group, head_dim), jnp.bfloat16)

    def rows_of(array, r):
        return array[r * group : (r + 1) * group]

    def attend(r, n):
        wide = jnp.concatenate(
            [
                jnp.concatenate([query[r, n], zero], axis=1),
                jnp.concatenate([zero, query[r, n + 1]], axis=1),
            ],
            axis=0,
        )
        at = r * nk + n
        scores = dot_t(wide, jnp.concatenate([keys_v[at], keys_v[at + 1]], axis=1))
        scores = jnp.concatenate(
            [
                jnp.where(spot < lengths[per * behind(n + k) + r], rows_of(scores, k), NEG)
                for k in range(2)
            ],
            axis=0,
        )
        mixed, stat = softmax_part(
            scores, jnp.concatenate([values_v[at], values_v[at + 1]], axis=1)
        )
        return [
            (rows_of(mixed, k)[:, k * head_dim : (k + 1) * head_dim], rows_of(stat, k))
            for k in range(2)
        ]

    for r in range(per):
        for b, (low, high) in enumerate(stages[r]):
            slots = range(low, high)
            away = slots[1:] if low == 0 else slots
            drain(query.at[r, pl.ds(away[0], len(away))], query_rs.at[steps * r + b])
            block = pl.ds(r * nk + low, high - low)
            drain(keys_v.at[block], key_sem.at[steps * r + b])
            drain(values_v.at[block], value_sem.at[steps * r + b])
            results = [part_of for n in slots[::2] for part_of in attend(r, n)]
            for n, (mixed, stat) in zip(slots, results):
                attn[r, n] = mixed.astype(jnp.bfloat16)
                if r == 0:
                    lse[n] = column_to_row(stat, 0)
                else:
                    lse[n] = lse[n] + column_to_row(stat, group)
            for n in reversed(away):
                send(attn.at[r, n], attn_in.at[r, n - 1], attn_ss, attn_rs, {"kv": behind(n)})
                if r == per - 1:
                    send(lse.at[n], lse_in.at[n - 1], lse_ss, lse_rs, {"kv": behind(n)})

    drain(lse_in, lse_rs)
    stats = jnp.concatenate([lse[0], fresh_lse] + [lse_in[n] for n in range(nk - 1)], axis=0)
    ratio = jnp.exp2(stats - jnp.max(stats, axis=0, keepdims=True))
    ratio = ratio / jnp.sum(ratio, axis=0, keepdims=True)
    ratio = jnp.concatenate([ratio, jnp.zeros((128 - nk - 1, 128), jnp.float32)], axis=0).T
    ratio = ratio[: per * group]
    merged = attn[:, 0].astype(jnp.float32).reshape(per * group, head_dim) * ratio[:, 0:1] + fresh_out * ratio[:, 1:2]
    drain(attn_in, attn_rs)
    for n in range(nk - 1):
        piece = attn_in[:, n].astype(jnp.float32).reshape(per * group, head_dim)
        merged = merged + piece * ratio[:, n + 2 : n + 3]
    merged = jnp.swapaxes(merged.reshape(per, heads, drafts, head_dim), 0, 1)
    merged = merged.reshape(heads, own, head_dim)
    attended[me] = jnp.concatenate(
        [
            jnp.concatenate([merged[h + k * heads // 2] for h in range(heads // 2)], axis=1)
            for k in range(2)
        ],
        axis=0,
    ).astype(jnp.bfloat16)
    for n in reversed(range(1, nk)):
        send(attended.at[me], attended.at[me], att_ss, att_rs, {"kv": ahead(n)})
    drain(attended.at[pl.ds(0, nk - 1)], att_rs)

    everyone = attended[...].reshape(nk * 2 * own, heads * head_dim // 2)
    total = None
    for k in range(2):
        half = pl.ds(k * heads * head_dim // 2, heads * head_dim // 2)
        term = dot_t(everyone, wo_v[:, half]).reshape(nk, 2, own, -1)[:, k]
        total = term if total is None else total + term
    width = out.shape[1]
    spare = jnp.zeros((rows, proj.shape[2] - width), jnp.float32)
    total = jnp.concatenate([total.reshape(rows, width), spare], axis=1)
    proj[...] = total.astype(jnp.bfloat16).reshape(proj.shape)
    for s in range(1, nh):
        target = lax.rem(my_head + s, nh)
        send(proj.at[target], proj_in.at[s - 1], proj_ss, proj_rs, {"head": target})
    drain(proj_in, proj_rs)
    result = proj[my_head].astype(jnp.float32)
    for s in range(nh - 1):
        result = result + proj_in[s].astype(jnp.float32)
    out[...] = result[:, :width].astype(jnp.bfloat16)

    drain(part_in, part_ss)
    drain(fresh_in, fresh_ss)
    drain(attn_in, query_ss)
    drain(attn_in, attn_ss)
    drain(lse_in, lse_ss)
    drain(attended.at[pl.ds(0, nk - 1)], att_ss)
    drain(proj_in, proj_ss)


def on_device(
    nk, nh,
    tokens, q_weight, key_matrix, value_matrix, q_gain, k_gain, keys, values, lengths, positions,
    o_weight,
):
    rows = tokens.shape[0]
    reqs, drafts = positions.shape
    width = o_weight.shape[1]
    tokens, o_weight, positions = tokens.T, o_weight.T, positions.T
    _, local_len, _, head_dim = keys.shape
    keys = keys.reshape(reqs, local_len, head_dim)
    values = values.reshape(reqs, local_len, head_dim)
    heads = q_gain.shape[0]
    side = math.isqrt(nk)
    own = rows // nk
    per = reqs // nk
    group = heads * drafts
    block = rows // nh
    padded = -(-width // 128) * 128
    exponent = np.arange(head_dim // 2, dtype=np.float64) * 2.0 / head_dim
    freq = np.tile((ROPE_BASE ** -exponent).astype(np.float32), 2)[None]
    bf16, f32 = jnp.bfloat16, jnp.float32
    dma = pltpu.SemaphoreType.DMA
    hbm = pl.BlockSpec(memory_space=pltpu.HBM)
    return pl.pallas_call(
        functools.partial(kernel, nk, side, nh, drafts),
        out_shape=jax.ShapeDtypeStruct((block, width), bf16),
        in_specs=[hbm] * 12,
        out_specs=pl.BlockSpec(memory_space=pltpu.VMEM),
        scratch_shapes=[
            pltpu.VMEM(tokens.shape, bf16),
            pltpu.VMEM(q_weight.shape, bf16),
            pltpu.VMEM(key_matrix.shape, bf16),
            pltpu.VMEM(value_matrix.shape, bf16),
            pltpu.VMEM(q_gain.shape, f32),
            pltpu.VMEM(k_gain.shape, f32),
            pltpu.VMEM(o_weight.shape, bf16),
            pltpu.VMEM(freq.shape, f32),
            pltpu.VMEM(keys.shape, bf16),
            pltpu.VMEM(values.shape, bf16),
            pltpu.SMEM(lengths.shape, jnp.int32),
            pltpu.SMEM(positions.shape, jnp.int32),
            pltpu.VMEM((per, nk, group, head_dim), f32),
            pltpu.VMEM((per, nk - 1, group, head_dim), f32),
            pltpu.VMEM((nk, 2 * own, head_dim), f32),
            pltpu.VMEM((nk - 1, 2 * own, head_dim), f32),
            pltpu.VMEM((per, nk, group, head_dim), bf16),
            pltpu.VMEM((per, nk, group, head_dim), bf16),
            pltpu.VMEM((per, nk - 1, group, head_dim), bf16),
            pltpu.VMEM((nk, 1, 128), f32),
            pltpu.VMEM((nk - 1, 1, 128), f32),
            pltpu.VMEM((nk, 2 * own, heads * head_dim // 2), bf16),
            pltpu.VMEM((nh, block, padded), bf16),
            pltpu.VMEM((nh - 1, block, padded), bf16),
            dma((10,)),
            dma((3 * per,)),
            dma((3 * per,)),
            dma((per,)),
            dma((3 * per,)),
            dma((12,)),
        ],
        compiler_params=pltpu.CompilerParams(
            collective_id=0, has_side_effects=True, vmem_limit_bytes=60 * 1024 * 1024
        ),
    )(
        tokens, q_weight, key_matrix, value_matrix, q_gain, k_gain, keys, values, o_weight,
        jnp.asarray(freq), lengths, positions,
    )


def solution(mesh):
    placed = (
        P(None, "kv"),
        P("kv", "head"),
        P("kv", "head"),
        P("kv", "head"),
        P("head", None),
        P("head", None),
        P(None, "kv", "head", None),
        P(None, "kv", "head", None),
        P(),
        P(),
        P("head", "kv"),
    )
    return jax.shard_map(
        functools.partial(on_device, mesh.shape["kv"], mesh.shape["head"]),
        mesh=mesh,
        in_specs=placed,
        out_specs=P("head", "kv"),
        check_vma=False,
    )
```

```python
import functools
import math

import jax
import jax.numpy as jnp
import numpy as np
from jax import lax
from jax.experimental import pallas as pl
from jax.experimental.pallas import tpu as pltpu
from jax.sharding import PartitionSpec as P

EPSILON = 1e-06
ROPE_BASE = 1000000.0
NEG = -1e30
MESH = pl.DeviceIdType.MESH


def column_to_row(col, first):
    rows = col.shape[0]
    wide = jnp.broadcast_to(col, (rows, 128))
    row_id = lax.broadcasted_iota(jnp.int32, (rows, 128), 0)
    lane_id = lax.broadcasted_iota(jnp.int32, (rows, 128), 1)
    return jnp.sum(jnp.where(row_id + first == lane_id, wide, 0.0), axis=0, keepdims=True)


def by_distance(side):
    spots = [(y, x) for y in range(side) for x in range(side)]
    return sorted(spots, key=lambda at: sum(min(d, side - d) for d in at))


def drain(ref, sem):
    pltpu.make_async_copy(ref, ref, sem).wait()


def kernel(
    nk, side, nh, drafts,
    tokens, q_weight, key_matrix, value_matrix, q_gain, k_gain, keys, values, o_weight, freq,
    lengths_in, positions_in,
    out,
    tok_v, wq_v, wk_v, wv_v, qg_v, kg_v, wo_v, freq_v, keys_v, values_v, lengths, positions,
    part, part_in, fresh, fresh_in, query, attn, attn_in, lse, lse_in, attended, proj, proj_in,
    load_sem, key_sem, value_sem, part_rs, query_rs, sems,
):
    (part_ss, fresh_ss, fresh_rs, query_ss, attn_ss, attn_rs, lse_ss, lse_rs, att_ss, att_rs,
     proj_ss, proj_rs) = [sems.at[n] for n in range(12)]
    me = lax.axis_index("kv")
    my_head = lax.axis_index("head")
    my_y, my_x = me // side, me % side
    reqs, local_len, head_dim = keys.shape
    rows = tokens.shape[1]
    heads = q_gain.shape[0]
    per = reqs // nk
    own = per * drafts
    group = heads * drafts
    scale = 1.0 / math.sqrt(head_dim)
    to_log2 = scale * math.log2(math.e)
    order = by_distance(side)
    quarter = max(nk // 4, 2)
    spans = [(0, quarter), (quarter, 2 * quarter), (2 * quarter, nk)]
    spans = [span for span in spans if span[0] < span[1]]
    stages = [spans, spans[::-1]]
    steps = len(stages[0])

    def ahead(n):
        y, x = order[n]
        return lax.rem(my_y + y, side) * side + lax.rem(my_x + x, side)

    def behind(n):
        y, x = order[n]
        return lax.rem(my_y + side - y, side) * side + lax.rem(my_x + side - x, side)

    def send(src, dst, send_sem, recv_sem, to):
        pltpu.make_async_remote_copy(
            src_ref=src, dst_ref=dst, send_sem=send_sem, recv_sem=recv_sem,
            device_id=to, device_id_type=MESH,
        ).start()

    barrier = pltpu.get_barrier_semaphore()
    for n in reversed(range(1, nk)):
        pl.semaphore_signal(barrier, inc=1, device_id={"kv": ahead(n)}, device_id_type=MESH)
    for s in range(1, nh):
        pl.semaphore_signal(
            barrier, inc=1, device_id={"head": lax.rem(my_head + s, nh)}, device_id_type=MESH
        )

    loads = [
        pltpu.make_async_copy(src, dst, load_sem.at[n])
        for n, (src, dst) in enumerate(
            [
                (tokens, tok_v), (q_weight, wq_v), (key_matrix, wk_v), (value_matrix, wv_v),
                (q_gain, qg_v), (k_gain, kg_v), (freq, freq_v), (o_weight, wo_v),
                (lengths_in, lengths), (positions_in, positions),
            ]
        )
    ]
    for copy in loads[:4]:
        copy.start()
    for copy in loads[:4]:
        copy.wait()
    toks = tok_v[...].T

    upper = lax.broadcasted_iota(jnp.int32, (rows, head_dim), 0) % own < drafts

    def split(first, second):
        low = jnp.where(upper, first, pltpu.roll(second, drafts, 0))
        high = jnp.where(upper, pltpu.roll(first, rows - drafts, 0), second)
        return [low.reshape(nk, own, head_dim), high.reshape(nk, own, head_dim)]

    for h in range(0, heads, 2):
        weight = wq_v[:, h * head_dim : (h + 2) * head_dim]
        both = jnp.dot(toks, weight, preferred_element_type=jnp.float32)
        for r, piece in enumerate(split(both[:, :head_dim], both[:, head_dim:])):
            part[r, :, h * drafts : (h + 2) * drafts, :] = piece
    weight = jnp.concatenate([wk_v[...], wv_v[...]], axis=1)
    both = jnp.dot(toks, weight, preferred_element_type=jnp.float32)
    fresh[...] = jnp.concatenate(
        [both[:, k * head_dim : (k + 1) * head_dim].reshape(nk, own, head_dim) for k in range(2)],
        axis=1,
    )

    pl.semaphore_wait(barrier, nk + nh - 2)

    for r in range(per):
        for n in range(1, nk):
            send(
                part.at[r, ahead(n)], part_in.at[r, n - 1], part_ss, part_rs.at[r],
                {"kv": ahead(n)},
            )
    for n in range(1, nk):
        send(fresh.at[ahead(n)], fresh_in.at[n - 1], fresh_ss, fresh_rs, {"kv": ahead(n)})

    for copy in loads[4:]:
        copy.start()
    for r in range(per):
        for b, (low, high) in enumerate(stages[r]):
            for n in range(low, high):
                at = per * behind(n) + r
                pltpu.make_async_copy(
                    keys.at[at], keys_v.at[r * nk + n], key_sem.at[steps * r + b]
                ).start()
                pltpu.make_async_copy(
                    values.at[at], values_v.at[r * nk + n], value_sem.at[steps * r + b]
                ).start()
    for copy in loads[4:]:
        copy.wait()
    row_id = lax.broadcasted_iota(jnp.int32, (own, head_dim), 0)
    lane_id = lax.broadcasted_iota(jnp.int32, (own, head_dim), 1)
    place = [[positions[j, per * me + r] for j in range(drafts)] for r in range(per)]
    place_rows = jnp.zeros((own, head_dim), jnp.int32)
    for r in range(per):
        for j in range(drafts):
            place_rows = jnp.where(row_id == r * drafts + j, place[r][j], place_rows)
    angle = place_rows.astype(jnp.float32) * freq_v[...]
    cosine = jnp.cos(angle)
    sine = jnp.sin(angle)
    sine = jnp.where(lane_id < head_dim // 2, -sine, sine)
    fresh_row = lax.broadcasted_iota(jnp.int32, (per * group, 16), 0)
    fresh_col = lax.broadcasted_iota(jnp.int32, (per * group, 16), 1)
    seen = fresh_row < 0
    for r in range(per):
        for j in range(drafts):
            here = (fresh_row // group == r) & (fresh_row % drafts == j)
            for i in range(j + 1):
                hit = here & (fresh_col == r * drafts + i)
                if i < j:
                    hit = hit & (place[r][i] < place[r][j])
                seen = seen | hit

    top_half = row_id < drafts

    def spread(array, r):
        turned = pltpu.roll(array, drafts, 0)
        return jnp.where(top_half, array, turned) if r == 0 else jnp.where(top_half, turned, array)

    turns = [(spread(cosine, r)[None], spread(sine, r)[None]) for r in range(per)]
    gains = qg_v[...]
    gains = jnp.concatenate(
        [
            jnp.where(top_half, gains[h : h + 1], gains[h + 1 : h + 2])[None]
            for h in range(0, heads, 2)
        ],
        axis=0,
    )

    def norm_rotate(vec, gain, turn):
        vec = vec * lax.rsqrt(jnp.mean(vec * vec, axis=-1, keepdims=True) + EPSILON) * gain
        turned = pltpu.roll(vec.reshape(-1, head_dim), head_dim // 2, 1).reshape(vec.shape)
        return vec * turn[0] + turned * turn[1]

    queries = []
    for r in range(per):
        drain(part_in.at[r], part_rs.at[r])
        raw = part[r, me]
        for n in range(nk - 1):
            raw = raw + part_in[r, n]
        mine = norm_rotate(raw.reshape(heads // 2, own, head_dim), gains, turns[r])
        mine = mine.reshape(group, head_dim).astype(jnp.bfloat16)
        queries.append(mine)
        query[r, 0] = mine
        for b, (low, high) in enumerate(stages[r]):
            for n in range(max(low, 1), high):
                send(
                    query.at[r, 0], query.at[r, n], query_ss, query_rs.at[steps * r + b],
                    {"kv": ahead(n)},
                )
    def softmax_part(scores, vals):
        top = jnp.max(scores, axis=-1, keepdims=True)
        weights = jnp.exp2((scores - top) * to_log2)
        total = jnp.sum(weights, axis=-1, keepdims=True)
        mixed = jnp.dot(weights.astype(jnp.bfloat16), vals, preferred_element_type=jnp.float32)
        return mixed / total, top * to_log2 + jnp.log2(total)

    def dot_t(left, right):
        return lax.dot_general(
            left, right, (((1,), (1,)), ((), ())), preferred_element_type=jnp.float32
        )

    queries = jnp.concatenate(queries, axis=0)

    drain(fresh_in, fresh_rs)
    fresh_kv = fresh[me]
    for n in range(nk - 1):
        fresh_kv = fresh_kv + fresh_in[n]
    fresh_k = norm_rotate(fresh_kv[:own][None], kg_v[...], (cosine[None], sine[None]))
    pad = jnp.zeros((16 - own, head_dim), jnp.float32)
    fresh_k = jnp.concatenate([fresh_k.reshape(own, head_dim), pad], axis=0).astype(jnp.bfloat16)
    fresh_v = jnp.concatenate([fresh_kv[own:], pad], axis=0).astype(jnp.bfloat16)

    fresh_out, fresh_lse = softmax_part(
        jnp.where(seen, dot_t(queries, fresh_k), NEG), fresh_v
    )
    fresh_lse = column_to_row(fresh_lse, 0)

    spot = me * local_len + lax.broadcasted_iota(jnp.int32, (1, local_len), 1)
    zero = jnp.zeros((group, head_dim), jnp.bfloat16)

    def rows_of(array, r):
        return array[r * group : (r + 1) * group]

    def attend(r, n):
        wide = jnp.concatenate(
            [
                jnp.concatenate([query[r, n], zero], axis=1),
                jnp.concatenate([zero, query[r, n + 1]], axis=1),
            ],
            axis=0,
        )
        at = r * nk + n
        scores = dot_t(wide, jnp.concatenate([keys_v[at], keys_v[at + 1]], axis=1))
        scores = jnp.concatenate(
            [
                jnp.where(spot < lengths[per * behind(n + k) + r], rows_of(scores, k), NEG)
                for k in range(2)
            ],
            axis=0,
        )
        mixed, stat = softmax_part(
            scores, jnp.concatenate([values_v[at], values_v[at + 1]], axis=1)
        )
        return [
            (rows_of(mixed, k)[:, k * head_dim : (k + 1) * head_dim], rows_of(stat, k))
            for k in range(2)
        ]

    for r in range(per):
        for b, (low, high) in enumerate(stages[r]):
            slots = range(low, high)
            away = slots[1:] if low == 0 else slots
            drain(query.at[r, pl.ds(away[0], len(away))], query_rs.at[steps * r + b])
            block = pl.ds(r * nk + low, high - low)
            drain(keys_v.at[block], key_sem.at[steps * r + b])
            drain(values_v.at[block], value_sem.at[steps * r + b])
            results = [part_of for n in slots[::2] for part_of in attend(r, n)]
            for n, (mixed, stat) in zip(slots, results):
                attn[r, n] = mixed.astype(jnp.bfloat16)
                if r == 0:
                    lse[n] = column_to_row(stat, 0)
                else:
                    lse[n] = lse[n] + column_to_row(stat, group)
            for n in reversed(away) if r == per - 1 else ():
                send(lse.at[n], lse_in.at[n - 1], lse_ss, lse_rs, {"kv": behind(n)})
            for n in reversed(away):
                send(attn.at[r, n], attn_in.at[r, n - 1], attn_ss, attn_rs, {"kv": behind(n)})

    drain(lse_in, lse_rs)
    stats = jnp.concatenate([lse[0], fresh_lse] + [lse_in[n] for n in range(nk - 1)], axis=0)
    ratio = jnp.exp2(stats - jnp.max(stats, axis=0, keepdims=True))
    ratio = ratio / jnp.sum(ratio, axis=0, keepdims=True)
    ratio = jnp.concatenate([ratio, jnp.zeros((128 - nk - 1, 128), jnp.float32)], axis=0).T
    ratio = ratio[: per * group]
    merged = attn[:, 0].astype(jnp.float32).reshape(per * group, head_dim) * ratio[:, 0:1] + fresh_out * ratio[:, 1:2]
    drain(attn_in, attn_rs)
    for n in range(nk - 1):
        piece = attn_in[:, n].astype(jnp.float32).reshape(per * group, head_dim)
        merged = merged + piece * ratio[:, n + 2 : n + 3]
    merged = jnp.swapaxes(merged.reshape(per, heads, drafts, head_dim), 0, 1)
    merged = merged.reshape(heads, own, head_dim)
    attended[me] = jnp.concatenate(
        [
            jnp.concatenate([merged[h + k * heads // 2] for h in range(heads // 2)], axis=1)
            for k in range(2)
        ],
        axis=0,
    ).astype(jnp.bfloat16)
    for n in reversed(range(1, nk)):
        send(attended.at[me], attended.at[me], att_ss, att_rs, {"kv": ahead(n)})
    drain(attended.at[pl.ds(0, nk - 1)], att_rs)

    everyone = attended[...].reshape(nk * 2 * own, heads * head_dim // 2)
    total = None
    for k in range(2):
        half = pl.ds(k * heads * head_dim // 2, heads * head_dim // 2)
        term = dot_t(everyone, wo_v[:, half]).reshape(nk, 2, own, -1)[:, k]
        total = term if total is None else total + term
    width = out.shape[1]
    spare = jnp.zeros((rows, proj.shape[2] - width), jnp.float32)
    total = jnp.concatenate([total.reshape(rows, width), spare], axis=1)
    proj[...] = total.astype(jnp.bfloat16).reshape(proj.shape)
    for s in sorted(range(1, nh), key=lambda s: abs(s - nh // 2)):
        target = lax.rem(my_head + s, nh)
        send(proj.at[target], proj_in.at[s - 1], proj_ss, proj_rs, {"head": target})
    drain(proj_in, proj_rs)
    result = proj[my_head].astype(jnp.float32)
    for s in range(nh - 1):
        result = result + proj_in[s].astype(jnp.float32)
    out[...] = result[:, :width].astype(jnp.bfloat16)

    drain(part_in, part_ss)
    drain(fresh_in, fresh_ss)
    drain(attn_in, query_ss)
    drain(attn_in, attn_ss)
    drain(lse_in, lse_ss)
    drain(attended.at[pl.ds(0, nk - 1)], att_ss)
    drain(proj_in, proj_ss)


def on_device(
    nk, nh,
    tokens, q_weight, key_matrix, value_matrix, q_gain, k_gain, keys, values, lengths, positions,
    o_weight,
):
    rows = tokens.shape[0]
    reqs, drafts = positions.shape
    width = o_weight.shape[1]
    tokens, o_weight, positions = tokens.T, o_weight.T, positions.T
    _, local_len, _, head_dim = keys.shape
    keys = keys.reshape(reqs, local_len, head_dim)
    values = values.reshape(reqs, local_len, head_dim)
    heads = q_gain.shape[0]
    side = math.isqrt(nk)
    own = rows // nk
    per = reqs // nk
    group = heads * drafts
    block = rows // nh
    padded = -(-width // 128) * 128
    exponent = np.arange(head_dim // 2, dtype=np.float64) * 2.0 / head_dim
    freq = np.tile((ROPE_BASE ** -exponent).astype(np.float32), 2)[None]
    bf16, f32 = jnp.bfloat16, jnp.float32
    dma = pltpu.SemaphoreType.DMA
    hbm = pl.BlockSpec(memory_space=pltpu.HBM)
    return pl.pallas_call(
        functools.partial(kernel, nk, side, nh, drafts),
        out_shape=jax.ShapeDtypeStruct((block, width), bf16),
        in_specs=[hbm] * 12,
        out_specs=pl.BlockSpec(memory_space=pltpu.VMEM),
        scratch_shapes=[
            pltpu.VMEM(tokens.shape, bf16),
            pltpu.VMEM(q_weight.shape, bf16),
            pltpu.VMEM(key_matrix.shape, bf16),
            pltpu.VMEM(value_matrix.shape, bf16),
            pltpu.VMEM(q_gain.shape, f32),
            pltpu.VMEM(k_gain.shape, f32),
            pltpu.VMEM(o_weight.shape, bf16),
            pltpu.VMEM(freq.shape, f32),
            pltpu.VMEM(keys.shape, bf16),
            pltpu.VMEM(values.shape, bf16),
            pltpu.SMEM(lengths.shape, jnp.int32),
            pltpu.SMEM(positions.shape, jnp.int32),
            pltpu.VMEM((per, nk, group, head_dim), f32),
            pltpu.VMEM((per, nk - 1, group, head_dim), f32),
            pltpu.VMEM((nk, 2 * own, head_dim), f32),
            pltpu.VMEM((nk - 1, 2 * own, head_dim), f32),
            pltpu.VMEM((per, nk, group, head_dim), bf16),
            pltpu.VMEM((per, nk, group, head_dim), bf16),
            pltpu.VMEM((per, nk - 1, group, head_dim), bf16),
            pltpu.VMEM((nk, 1, 128), f32),
            pltpu.VMEM((nk - 1, 1, 128), f32),
            pltpu.VMEM((nk, 2 * own, heads * head_dim // 2), bf16),
            pltpu.VMEM((nh, block, padded), bf16),
            pltpu.VMEM((nh - 1, block, padded), bf16),
            dma((10,)),
            dma((3 * per,)),
            dma((3 * per,)),
            dma((per,)),
            dma((3 * per,)),
            dma((12,)),
        ],
        compiler_params=pltpu.CompilerParams(
            collective_id=0, has_side_effects=True, vmem_limit_bytes=60 * 1024 * 1024
        ),
    )(
        tokens, q_weight, key_matrix, value_matrix, q_gain, k_gain, keys, values, o_weight,
        jnp.asarray(freq), lengths, positions,
    )


def solution(mesh):
    placed = (
        P(None, "kv"),
        P("kv", "head"),
        P("kv", "head"),
        P("kv", "head"),
        P("head", None),
        P("head", None),
        P(None, "kv", "head", None),
        P(None, "kv", "head", None),
        P(),
        P(),
        P("head", "kv"),
    )
    return jax.shard_map(
        functools.partial(on_device, mesh.shape["kv"], mesh.shape["head"]),
        mesh=mesh,
        in_specs=placed,
        out_specs=P("head", "kv"),
        check_vma=False,
    )
```
